256 devices in a mesh: dp: 32 (over x, z), tensor: 8 (over y, core).
Axes of the slice: x: 4, y: 4, z: 8, core: 2. Of those that a mesh axis runs over, the one named last changes fastest.
Arguments:
- momentum: float32 [32, 8192, 1024], P('dp', None, 'tensor'), may hold values from -6 to 6
- gradient: bfloat16 [32, 8192, 1024], P('dp', None, 'tensor'), may hold values from -6 to 6
- masters: float32 [8192, 1024], P('dp', 'tensor'), may hold values from -6 to 6
- tokens: bfloat16 [4096, 8192], P('dp', 'tensor'), may hold values from -6 to 6
- freq_index: int32 [8, 1024], P('tensor'), may hold values from 0 to 8191, as said below
Outputs:
- residual: float32 [32, 8192, 1024], P('dp', None, 'tensor')
- new_masters: float32 [8192, 1024], P('dp', 'tensor')
- keys_out: bfloat16 [4096, 1024], P('dp', 'tensor')
The draws below stay inside these ranges and needn't reach their ends.
Inputs may be any that keep to these rules, and one draw needn't show every extreme that they name: `freq_index`: each row lists 1024 distinct frequencies, 0 and 8191 among them; the same list serves every replica.
All inputs are finite; a program needn't handle non-finite values.
Results may differ from the reference program's by a relative error of at most 0.007.
Values may be sent and summed in bfloat16 or wider, within the bound.
A program may use at most 64 MiB of HBM per device.

```python
import math
import jax
import jax.numpy as jnp
from jax import lax

D = 8192
COLS = 1024
CB = 128
FREQS = 1024
BLOCKS = 8
REPLICAS = 32
TOKENS = 4096


def draw_freq_index(key, part):
    keys = jax.random.split(key, BLOCKS)

    def one_block(block_key):
        pick_key, order_key = jax.random.split(block_key)
        chosen = jax.random.permutation(pick_key, D - 2)[:FREQS - 2] + 1
        listed = jnp.concatenate([jnp.array([0, D - 1], jnp.int32), chosen.astype(jnp.int32)])
        return listed[jax.random.permutation(order_key, FREQS)]
    return jax.vmap(one_block)(keys)


def steps_of(stream_key, shape, pieces, least, top_value):
    gain = 1.0
    for dim, blocks in pieces:
        steps = jax.random.uniform(jax.random.fold_in(jax.random.fold_in(stream_key, 6), dim), (blocks,), jnp.float32, least / len(pieces), top_value / len(pieces))
        gain = gain * jnp.repeat(jnp.exp(steps), shape[dim] // blocks).reshape((-1,) + (1,) * (len(shape) - 1 - dim))
    return gain


def normal_values(stream_key, shape, scale, limit, cuts=(), kind=jnp.bfloat16):
    entries = jax.random.normal(stream_key, shape, jnp.float32) * scale
    if len(cuts) > 0:
        entries = steps_of(stream_key, shape, cuts, -0.22, 0.18) * entries
    return jnp.clip(entries, min=-limit, max=limit).astype(kind)


def setup_inputs(seed: int = 0) -> dict:
    streams_of = jax.random.split(jax.random.key(seed), 6)
    momentum = normal_values(streams_of[0], (REPLICAS, D, COLS), 1.0, 6.0, ((0, 32), (2, 8)), jnp.float32)
    gradient = normal_values(streams_of[1], (REPLICAS, D, COLS), 1.0, 6.0, ((0, 32), (2, 8)))
    masters = normal_values(streams_of[2], (D, COLS), 1.0, 6.0, ((0, 32), (1, 8)), jnp.float32)
    tokens = normal_values(streams_of[3], (TOKENS, D), 1.0, 6.0, ((0, 32), (1, 8)))
    freq_index = draw_freq_index(jax.random.fold_in(streams_of[5], 71), 0)
    return {"momentum": momentum, "gradient": gradient, "masters": masters, "tokens": tokens, "freq_index": freq_index}


momentum_decay = 0.9
step_rate = 1.0

def cosine_rows(frequency, first_row, row_count, model_width):
    positions = first_row + lax.iota(jnp.int32, row_count)
    phases = (2 * positions + 1)[None, :] * frequency[:, None] % (4 * model_width)
    angles = phases.astype(jnp.float32) * (math.pi / (2 * model_width))
    scales = jnp.where(frequency == 0, math.sqrt(1.0 / model_width), math.sqrt(2.0 / model_width)).astype(jnp.float32)
    return (scales[:, None] * jnp.cos(angles)).astype(jnp.bfloat16)

def reference(momentum, gradient, masters, tokens, freq_index):
    replicas = momentum.shape[0]
    remains = []
    updates = []
    highest = lax.Precision.HIGHEST
    for column_block in range(COLS // CB):
        lower = column_block * CB
        cosines = cosine_rows(freq_index[column_block], 0, D, D)

        def replica_step(summed, inputs):
            moment_rows, grad_rows = inputs
            states = momentum_decay * moment_rows + grad_rows.astype(jnp.float32)
            coefficient = jnp.dot(cosines, states.astype(jnp.bfloat16), preferred_element_type=jnp.float32).astype(jnp.bfloat16)
            remain = states - jnp.dot(cosines.T, coefficient, preferred_element_type=jnp.float32)
            return (summed + coefficient.astype(jnp.float32), remain)
        summed, remain = lax.scan(replica_step, jnp.zeros((FREQS, CB), jnp.float32), (momentum[:, :, lower:lower + CB], gradient[:, :, lower:lower + CB]))
        remains.append(remain)
        updates.append(jnp.dot(cosines.astype(jnp.float32).T, summed / replicas, precision=highest))
    residual = jnp.concatenate(remains, axis=2)
    update = jnp.concatenate(updates, axis=1)
    new_masters = masters - step_rate * update
    weights = new_masters.astype(jnp.bfloat16)
    projected = jnp.dot(tokens, weights, preferred_element_type=jnp.float32) * D ** (-0.5)
    return (residual, new_masters, projected.astype(jnp.bfloat16))
```

```python
import math

import jax
import jax.numpy as jnp
from jax import lax
from jax.experimental import pallas as pl
from jax.experimental.pallas import tpu as pltpu
from jax.sharding import PartitionSpec as P

D = 8192
H = D // 2
K = 1024
CB = 128
X, Z = 4, 8
REPLICAS = X * Z
R = 256
T = 128
RA = 160
RB = R - RA
BF = jnp.bfloat16
F32 = jnp.float32

TOK, AR, AL, AX, BX, BR, BL, CX, CZ, GZ, GX, MSGS = 0, 8, 12, 15, 19, 23, 26, 30, 33, 40, 47, 50


def dot(a, b):
    return jnp.dot(a, b, preferred_element_type=F32)


def dot_nt(a, b):
    return lax.dot_general(a, b, (((1,), (1,)), ((), ())), preferred_element_type=F32)


def cos_sin(phase):
    quadrant = (phase + 4096) >> 13
    angle = (phase - (quadrant << 13)).astype(F32) * (math.pi / 16384)
    square = angle * angle
    sine = angle * (1.0 + square * (-1 / 6 + square * (1 / 120 + square * (-1 / 5040))))
    cosine = 1.0 + square * (-0.5 + square * (1 / 24 + square * (-1 / 720 + square * (1 / 40320))))
    swap = (quadrant & 1) == 1
    c = jnp.where(swap, sine, cosine)
    s = jnp.where(swap, cosine, sine)
    c = jnp.where(((quadrant + 1) & 2) == 2, -c, c)
    s = jnp.where((quadrant & 2) == 2, -s, s)
    return c, s


def kernel(mom, grad, mast, tok_in, freq, res, newm, keys,
           state, gbuf, table, xt, seo, coef, rsx, rszs, rszr, sbuf, tok, tt, left, wbuf, mbuf, fbuf,
           ca, sa, ldsem, stsem, ssem, rsem):
    i = lax.axis_index("dp")
    t = lax.axis_index("tensor")
    x, z = i // Z, i % Z
    y, core = t // 2, t % 2

    def xdev(d):
        return (((x + d) % X) * Z + z, t)

    def zdev(d):
        return (x * Z + (z + d) % Z, t)

    def ydev(d):
        return (i, ((y + d) % 4) * 2 + core)

    twin = (i, y * 2 + (1 - core))

    barrier = pltpu.get_barrier_semaphore()
    peers = [xdev(d) for d in range(1, X)] + [zdev(d) for d in range(1, Z)] + [ydev(1), ydev(3), twin]
    for peer in peers:
        pl.semaphore_signal(barrier, inc=1, device_id=peer, device_id_type=pl.DeviceIdType.MESH)

    load_mast = pltpu.make_async_copy(mast, mbuf, ldsem.at[0])
    load_freq = pltpu.make_async_copy(freq, fbuf, ldsem.at[1])
    load_tok = pltpu.make_async_copy(tok_in, tok.at[t], ldsem.at[2])
    load_mast.start()
    load_freq.start()
    load_tok.start()
    loads = []
    for c in (0, 7, 1, 6, 2, 5, 3, 4):
        rows = pl.ds(1024 * c, 1024)
        a = pltpu.make_async_copy(mom.at[0, rows], state.at[rows], ldsem.at[3 + c])
        b = pltpu.make_async_copy(grad.at[0, rows], gbuf.at[rows], ldsem.at[11 + c])
        a.start()
        b.start()
        loads.append((a, b))

    sent = []

    def send(number, src, dst, device):
        copy = pltpu.make_async_remote_copy(
            src_ref=src, dst_ref=dst, send_sem=ssem.at[number], recv_sem=rsem.at[number],
            device_id=device, device_id_type=pl.DeviceIdType.MESH)
        copy.start()
        sent.append(copy)

    def arrived(number, ref):
        pltpu.make_async_remote_copy(
            src_ref=ref, dst_ref=ref, send_sem=ssem.at[number], recv_sem=rsem.at[number],
            device_id=twin, device_id_type=pl.DeviceIdType.MESH).wait_recv()

    load_mast.wait()
    wbuf[x, z] = mbuf[...].astype(BF)
    load_tok.wait()
    pl.semaphore_wait(barrier, len(peers))

    def a_block(xx, zz):
        return wbuf.at[xx % X, zz % Z, pl.ds(0, RA)]

    def a_right(s):
        send(AR + s, a_block(x, z - s + Z), a_block(x, z - s + Z), zdev(1))

    def a_left(s):
        send(AL + s, a_block(x, z + s), a_block(x, z + s), zdev(-1 + Z))

    def a_right_in(s):
        arrived(AR + s, a_block(x, z - 1 - s + Z))

    def a_left_in(s):
        arrived(AL + s, a_block(x, z + 1 + s))

    def a_plane(xx, lo, n):
        return wbuf.at[xx % X, pl.ds(lo, n), pl.ds(0, RA)]

    def b_part(xx, lo, n):
        return wbuf.at[xx % X, z, pl.ds(RA + lo, n)]

    def b_plane(zz):
        return wbuf.at[:, zz % Z, pl.ds(RA, RB)]

    def b_right(s):
        send(BR + s, b_plane(z - s + Z), b_plane(z - s + Z), zdev(1))

    def b_left(s):
        send(BL + s, b_plane(z + s), b_plane(z + s), zdev(-1 + Z))

    def b_right_in(s):
        arrived(BR + s, b_plane(z - 1 - s + Z))

    def b_left_in(s):
        arrived(BL + s, b_plane(z + 1 + s))

    def tok_half(yy, lo, n):
        return tok.at[(yy % 4) * 2 + core, pl.ds(lo, n)]

    def tok_twin(yy):
        return tok.at[(yy % 4) * 2 + 1 - core]

    send(TOK + 0, tok_half(y, 0, T), tok_half(y, 0, T), ydev(1))
    send(TOK + 1, tok_half(y, 0, T), tok_half(y, 0, T), ydev(3))
    a_right(0)
    a_left(0)
    send(BX + 0, b_part(x, 0, RB), b_part(x, 0, RB), xdev(1))
    send(BX + 1, b_part(x, 0, RB), b_part(x, 0, RB), xdev(3))
    send(TOK + 2, tok_half(y, 0, T), tok_half(y, 0, T), twin)

    load_freq.wait()

    row = lax.broadcasted_iota(jnp.int32, (R, R), 0)
    col = lax.broadcasted_iota(jnp.int32, (R, R), 1)
    mirror = jnp.where(row + col == R - 1, 1.0, 0.0).astype(BF)
    unit = jnp.where(
        lax.broadcasted_iota(jnp.int32, (CB, CB), 0) == lax.broadcasted_iota(jnp.int32, (CB, CB), 1), 1.0, 0.0
    ).astype(BF)

    def odd_lanes(q):
        return (fbuf[:, pl.ds(pl.multiple_of(q * R, R), R)] & 1) == 1

    def build(q):
        counts = lax.broadcasted_iota(jnp.int32, (64, 128), 0)
        for h in range(2):
            f = fbuf[:, pl.ds(pl.multiple_of(q * R + h * 128, 128), 128)]
            scale = jnp.where(f == 0, math.sqrt(1.0 / D), math.sqrt(2.0 / D)).astype(F32)
            c, s = cos_sin((counts * 128 * f) & 32767)
            ca[...] = c * scale
            sa[...] = s * scale
            cb, sb = cos_sin(((2 * counts + 1) * f) & 32767)

            def step(a, carry):
                value = ca[pl.ds(a, 1)] * cb - sa[pl.ds(a, 1)] * sb
                table[q, pl.ds(pl.multiple_of(a * 64, 64), 64), pl.ds(h * 128, 128)] = value.astype(BF)
                return carry

            lax.fori_loop(0, 64, step, 0, unroll=4)

    def fold(j, carry):
        low = pl.ds(pl.multiple_of(j * R, R), R)
        high = pl.ds(pl.multiple_of(D - R - j * R, R), R)
        lows = 0.9 * state[low] + gbuf[low].astype(F32)
        highs = 0.9 * state[high] + gbuf[high].astype(F32)
        state[low] = lows
        state[high] = highs
        turned = dot(mirror, highs.astype(BF))
        xt[pl.ds(0, CB), low] = dot_nt(unit, (lows + turned).astype(BF)).astype(BF)
        xt[pl.ds(CB, CB), low] = dot_nt(unit, (lows - turned).astype(BF)).astype(BF)
        return carry

    def forward(q):
        both = dot(xt[...], table[q])
        odd = odd_lanes(q)
        own = jnp.where(odd, both[CB:], both[:CB]).astype(BF)
        coef[q] = own
        zero = jnp.zeros_like(own)
        seo[q, pl.ds(0, CB)] = jnp.where(odd, zero, own)
        seo[q, pl.ds(CB, CB)] = jnp.where(odd, own, zero)

    def inverse(j, carry):
        low = pl.ds(pl.multiple_of(j * R, R), R)
        high = pl.ds(pl.multiple_of(D - R - j * R, R), R)
        total = dot_nt(table[0, low], seo[0])
        for q in range(1, X):
            total += dot_nt(table[q, low], seo[q])
        even, odd = total[:, :CB], total[:, CB:]
        state[low] -= even + odd
        state[high] -= dot(mirror, (even - odd).astype(BF))
        pltpu.make_async_copy(state.at[low], res.at[0, low], stsem.at[2 * j]).start()
        pltpu.make_async_copy(state.at[high], res.at[0, high], stsem.at[2 * j + 1]).start()
        return carry

    def send_coef(d):
        send(CX + d - 1, coef.at[(x + d) % X], rsx.at[d - 1], xdev(d))

    build((x + 2) % X)
    for s in range(4):
        for a, b in loads[2 * s:2 * s + 2]:
            a.wait()
            b.wait()
        lax.fori_loop(4 * s, 4 * s + 4, fold, 0)
    a_right_in(0)
    a_right(1)
    a_left_in(0)
    a_left(1)
    arrived(BX + 0, b_part(x + 3, 0, RB))
    send(BX + 2, b_part(x + 3, 0, RB // 2), b_part(x + 3, 0, RB // 2), xdev(1))
    arrived(BX + 1, b_part(x + 1, 0, RB))
    send(BX + 3, b_part(x + 1, RB // 2, RB // 2), b_part(x + 1, RB // 2, RB // 2), xdev(3))
    forward((x + 2) % X)
    send_coef(2)
    build((x + 1) % X)
    a_right_in(1)
    a_right(2)
    a_left_in(1)
    a_left(2)
    arrived(BX + 2, b_part(x + 2, 0, RB // 2))
    arrived(BX + 3, b_part(x + 2, RB // 2, RB // 2))
    b_right(0)
    b_left(0)
    forward((x + 1) % X)
    send_coef(1)
    build((x + 3) % X)
    arrived(TOK + 0, tok_half(y + 3, 0, T))
    send(TOK + 3, tok_half(y + 3, 0, T // 2), tok_half(y + 3, 0, T // 2), ydev(1))
    send(TOK + 5, tok_half(y + 3, 0, T), tok_half(y + 3, 0, T), twin)
    arrived(TOK + 1, tok_half(y + 1, 0, T))
    send(TOK + 4, tok_half(y + 1, T // 2, T // 2), tok_half(y + 1, T // 2, T // 2), ydev(3))
    send(TOK + 6, tok_half(y + 1, 0, T), tok_half(y + 1, 0, T), twin)
    forward((x + 3) % X)
    send_coef(3)
    a_right_in(2)
    a_right(3)
    a_left_in(2)
    build(x)
    b_right_in(0)
    b_right(1)
    b_left_in(0)
    b_left(1)
    forward(x)

    total = coef[x].astype(F32)
    for d in range(1, X):
        arrived(CX + d - 1, rsx.at[d - 1])
    for d in range(1, X):
        total += rsx[d - 1].astype(F32)
    rszs[...] = total.astype(BF).reshape(Z, 16, R)
    for d in range(1, Z):
        send(CZ + d - 1, rszs.at[(z + d) % Z], rszr.at[d - 1], zdev(d))
    a_right_in(3)
    send(AX + 0, a_plane(x, 0, Z), a_plane(x, 0, Z), xdev(1))
    send(AX + 1, a_plane(x, 0, Z), a_plane(x, 0, Z), xdev(3))
    b_right_in(1)
    b_right(2)
    b_left_in(1)
    b_left(2)
    lax.fori_loop(0, 6, inverse, 0)
    for d in range(1, Z):
        arrived(CZ + d - 1, rszr.at[d - 1])
    part = rszs[z].astype(F32)
    for d in range(1, Z):
        part += rszr[d - 1].astype(F32)

    def s_rows(xx, zz):
        return sbuf.at[xx % X, pl.ds(pl.multiple_of((zz % Z) * 16, 16), 16)]

    sbuf[x, pl.ds(pl.multiple_of(z * 16, 16), 16)] = (part * (1.0 / REPLICAS)).astype(BF)
    for d in range(1, Z):
        send(GZ + d - 1, s_rows(x, z), s_rows(x, z), zdev(d))
    b_right_in(2)
    b_left_in(2)
    b_left(3)
    arrived(TOK + 3, tok_half(y + 2, 0, T // 2))
    arrived(TOK + 4, tok_half(y + 2, T // 2, T // 2))
    send(TOK + 7, tok_half(y + 2, 0, T), tok_half(y + 2, 0, T), twin)
    lax.fori_loop(6, 12, inverse, 0)
    for d in range(1, Z):
        arrived(GZ + d - 1, s_rows(x, z - d + Z))
    for d in range(1, X):
        send(GX + d - 1, sbuf.at[x], sbuf.at[x], xdev(d))
    lax.fori_loop(12, 16, inverse, 0)

    arrived(TOK + 2, tok_twin(y))
    arrived(TOK + 5, tok_twin(y + 3))
    arrived(TOK + 6, tok_twin(y + 1))
    arrived(TOK + 7, tok_twin(y + 2))
    for j in range(H // R):
        b, o = j // 4, j % 4
        lows = tok[b, :, o * R:(o + 1) * R].astype(F32)
        turned = dot(tok[7 - b, :, (3 - o) * R:(4 - o) * R], mirror)
        tt[0:T, j * R:(j + 1) * R] = (lows + turned).astype(BF)
        tt[T:2 * T, j * R:(j + 1) * R] = (lows - turned).astype(BF)
    second = i >= REPLICAS // 2
    place = jnp.where(second, REPLICAS - 1 - i, i)
    pick = jnp.where(col == jnp.where(second, R - 1 - row, row), 1.0, 0.0).astype(BF)

    def token_step(q, carry):
        both = dot(tt[...], table[q])
        odd = odd_lanes(q)
        left[q, pl.ds(R, T)] = jnp.where(odd, both[T:], both[:T]).astype(BF)
        own = dot(pick, table[q, pl.ds(pl.multiple_of(place * R, R), R)])
        left[q, pl.ds(0, R)] = jnp.where(jnp.logical_and(odd, second), -own, own).astype(BF)
        return carry

    lax.fori_loop(0, X, token_step, 0)

    arrived(AX + 0, a_plane(x + 3, 0, Z))
    send(AX + 2, a_plane(x + 3, 0, Z // 2), a_plane(x + 3, 0, Z // 2), xdev(1))
    arrived(AX + 1, a_plane(x + 1, 0, Z))
    send(AX + 3, a_plane(x + 1, Z // 2, Z // 2), a_plane(x + 1, Z // 2, Z // 2), xdev(3))
    b_left_in(3)

    product = dot_nt(left[x], sbuf[x])
    for d in range(1, X):
        arrived(GX + d - 1, sbuf.at[(x - d + X) % X])
        product += dot_nt(left[(x - d + X) % X], sbuf[(x - d + X) % X])
    newm[...] = mbuf[...] - product[:R]

    arrived(AX + 2, a_plane(x + 2, 0, Z // 2))
    arrived(AX + 3, a_plane(x + 2, Z // 2, Z // 2))
    found = -product[R:]
    for b in range(8):
        found += dot(tok[b], wbuf[b // 2, pl.ds((b % 2) * 4, 4)].reshape(1024, CB))
    keys[...] = (found * D ** -0.5).astype(BF)

    for copy in sent:
        copy.wait_send()

    def drain(j, carry):
        low = pl.ds(pl.multiple_of(j * R, R), R)
        high = pl.ds(pl.multiple_of(D - R - j * R, R), R)
        pltpu.make_async_copy(state.at[low], res.at[0, low], stsem.at[2 * j]).wait()
        pltpu.make_async_copy(state.at[high], res.at[0, high], stsem.at[2 * j + 1]).wait()
        return carry

    lax.fori_loop(0, H // R, drain, 0)


def body(momentum, gradient, masters, tokens, freq_index):
    hbm = pl.BlockSpec(memory_space=pl.ANY)
    vmem = pl.BlockSpec(memory_space=pltpu.VMEM)
    return pl.pallas_call(
        kernel,
        out_shape=(
            jax.ShapeDtypeStruct((1, D, CB), F32),
            jax.ShapeDtypeStruct((R, CB), F32),
            jax.ShapeDtypeStruct((T, CB), BF),
        ),
        in_specs=[hbm] * 5,
        out_specs=(hbm, vmem, vmem),
        scratch_shapes=[
            pltpu.VMEM((D, CB), F32),
            pltpu.VMEM((D, CB), BF),
            pltpu.VMEM((X, H, R), BF),
            pltpu.VMEM((2 * CB, H), BF),
            pltpu.VMEM((X, 2 * CB, R), BF),
            pltpu.VMEM((X, CB, R), BF),
            pltpu.VMEM((X - 1, CB, R), BF),
            pltpu.VMEM((Z, 16, R), BF),
            pltpu.VMEM((Z - 1, 16, R), BF),
            pltpu.VMEM((X, CB, R), BF),
            pltpu.VMEM((8, T, 1024), BF),
            pltpu.VMEM((2 * T, H), BF),
            pltpu.VMEM((X, R + T, R), BF),
            pltpu.VMEM((X, Z, R, CB), BF),
            pltpu.VMEM((R, CB), F32),
            pltpu.VMEM((1, K), jnp.int32),
            pltpu.VMEM((64, 128), F32),
            pltpu.VMEM((64, 128), F32),
            pltpu.SemaphoreType.DMA((19,)),
            pltpu.SemaphoreType.DMA((32,)),
            pltpu.SemaphoreType.DMA((MSGS,)),
            pltpu.SemaphoreType.DMA((MSGS,)),
        ],
        compiler_params=pltpu.CompilerParams(
            collective_id=0, has_side_effects=True, vmem_limit_bytes=56 * 1024 * 1024),
    )(momentum, gradient, masters, tokens, freq_index)


def solution(mesh):
    return jax.shard_map(
        body,
        mesh=mesh,
        in_specs=(
            P("dp", None, "tensor"),
            P("dp", None, "tensor"),
            P("dp", "tensor"),
            P("dp", "tensor"),
            P("tensor", None),
        ),
        out_specs=(P("dp", None, "tensor"), P("dp", "tensor"), P("dp", "tensor")),
        check_vma=False,
    )
```

```python
import math

import jax
import jax.numpy as jnp
from jax import lax
from jax.experimental import pallas as pl
from jax.experimental.pallas import tpu as pltpu
from jax.sharding import PartitionSpec as P

D = 8192
H = D // 2
K = 1024
CB = 128
X, Z = 4, 8
REPLICAS = X * Z
R = 256
T = 128
BF = jnp.bfloat16
F32 = jnp.float32

TOK, MZ, XP, XM, FP, FM, CX, CZ, GZ, GX, MSGS = 0, 8, 15, 23, 31, 35, 39, 42, 49, 56, 59
PASS_P, PASS_M = (0, 1, 2, 3), (7, 6, 5, 4)


def dot(a, b):
    return jnp.dot(a, b, preferred_element_type=F32)


def dot_nt(a, b):
    return lax.dot_general(a, b, (((1,), (1,)), ((), ())), preferred_element_type=F32)


def cos_sin(phase):
    quadrant = (phase + 4096) >> 13
    angle = (phase - (quadrant << 13)).astype(F32) * (math.pi / 16384)
    square = angle * angle
    sine = angle * (1.0 + square * (-1 / 6 + square * (1 / 120 + square * (-1 / 5040))))
    cosine = 1.0 + square * (-0.5 + square * (1 / 24 + square * (-1 / 720 + square * (1 / 40320))))
    swap = (quadrant & 1) == 1
    c = jnp.where(swap, sine, cosine)
    s = jnp.where(swap, cosine, sine)
    c = jnp.where(((quadrant + 1) & 2) == 2, -c, c)
    s = jnp.where((quadrant & 2) == 2, -s, s)
    return c, s


def kernel(mom, grad, mast, tok_in, freq, res, newm, keys,
           gbuf, table, xt, seo, coef, rsx, rszs, rszr, sbuf, tok, tt, left, wbuf, mbuf, fbuf, frel, acc,
           ca, sa, ldsem, ssem, rsem):
    i = lax.axis_index("dp")
    t = lax.axis_index("tensor")
    x, z = i // Z, i % Z
    y, core = t // 2, t % 2

    def xdev(d):
        return (((x + d) % X) * Z + z, t)

    def zdev(d):
        return (x * Z + (z + d) % Z, t)

    def ydev(d):
        return (i, ((y + d) % 4) * 2 + core)

    twin = (i, y * 2 + (1 - core))

    barrier = pltpu.get_barrier_semaphore()
    peers = [xdev(d) for d in range(1, X)] + [zdev(d) for d in range(1, Z)] + [ydev(1), ydev(3), twin]
    for peer in peers:
        pl.semaphore_signal(barrier, inc=1, device_id=peer, device_id_type=pl.DeviceIdType.MESH)

    load_mast = pltpu.make_async_copy(mast, mbuf, ldsem.at[0])
    load_freq = pltpu.make_async_copy(freq, fbuf, ldsem.at[1])
    load_tok = pltpu.make_async_copy(tok_in, tok.at[t], ldsem.at[2])
    load_mast.start()
    load_tok.start()
    load_freq.start()
    loads = []
    for c in (0, 7, 1, 6, 2, 5, 3, 4):
        rows = pl.ds(1024 * c, 1024)
        a = pltpu.make_async_copy(mom.at[0, rows], res.at[0, rows], ldsem.at[3 + c])
        b = pltpu.make_async_copy(grad.at[0, rows], gbuf.at[rows], ldsem.at[11 + c])
        a.start()
        b.start()
        loads.append((a, b))

    sent = []

    def send(number, src, dst, device):
        copy = pltpu.make_async_remote_copy(
            src_ref=src, dst_ref=dst, send_sem=ssem.at[number], recv_sem=rsem.at[number],
            device_id=device, device_id_type=pl.DeviceIdType.MESH)
        copy.start()
        sent.append(copy)

    def arrived(number, ref):
        pltpu.make_async_remote_copy(
            src_ref=ref, dst_ref=ref, send_sem=ssem.at[number], recv_sem=rsem.at[number],
            device_id=twin, device_id_type=pl.DeviceIdType.MESH).wait_recv()

    load_mast.wait()
    wbuf[x, z] = mbuf[...].astype(BF)
    load_tok.wait()
    pl.semaphore_wait(barrier, len(peers))

    def block(dx, dz):
        return wbuf.at[(x + dx) % X, (z + dz) % Z]

    def spread(dz):
        send(XP + dz, block(0, dz), block(0, dz), xdev(1))
        send(XM + dz, block(0, dz), block(0, dz), xdev(3))

    def from_z(*offsets):
        for dz in offsets:
            arrived(MZ + (Z - dz) - 1, block(0, dz))
            spread(dz)

    def from_x(*offsets):
        for dz in offsets:
            arrived(XP + dz, block(3, dz))
            if dz in PASS_P:
                send(FP + PASS_P.index(dz), block(3, dz), block(3, dz), xdev(1))
            arrived(XM + dz, block(1, dz))
            if dz in PASS_M:
                send(FM + PASS_M.index(dz), block(1, dz), block(1, dz), xdev(3))

    def tok_half(yy, lo, n):
        return tok.at[(yy % 4) * 2 + core, pl.ds(lo, n)]

    def tok_twin(yy):
        return tok.at[(yy % 4) * 2 + 1 - core]

    send(TOK + 0, tok_half(y, 0, T), tok_half(y, 0, T), ydev(1))
    send(TOK + 1, tok_half(y, 0, T), tok_half(y, 0, T), ydev(3))
    for d in (1, 7, 2, 6, 3, 5, 4):
        send(MZ + d - 1, block(0, 0), block(0, 0), zdev(d))
    spread(0)
    send(TOK + 2, tok_half(y, 0, T), tok_half(y, 0, T), twin)

    load_freq.wait()
    for d in range(X):
        frel[:, d * R:(d + 1) * R] = fbuf[:, pl.ds(pl.multiple_of(((x + d) % X) * R, R), R)]

    row = lax.broadcasted_iota(jnp.int32, (R, R), 0)
    col = lax.broadcasted_iota(jnp.int32, (R, R), 1)
    mirror = jnp.where(row + col == R - 1, 1.0, 0.0).astype(BF)
    unit = jnp.where(
        lax.broadcasted_iota(jnp.int32, (CB, CB), 0) == lax.broadcasted_iota(jnp.int32, (CB, CB), 1), 1.0, 0.0
    ).astype(BF)

    def angles(d):
        counts = lax.broadcasted_iota(jnp.int32, (64, 128), 0)
        waves = []
        for h in range(2):
            f = frel[:, d * R + h * 128:d * R + (h + 1) * 128]
            scale = jnp.where(f == 0, math.sqrt(1.0 / D), math.sqrt(2.0 / D)).astype(F32)
            c, s = cos_sin((counts * 128 * f) & 32767)
            ca[h] = c * scale
            sa[h] = s * scale
            waves.append(cos_sin(((2 * counts + 1) * f) & 32767))
        return waves

    def build(d, b, waves):
        base = pl.multiple_of(b * 1024, 1024)
        for n in range(16):
            for h in range(2):
                cb, sb = waves[h]
                value = ca[h, pl.ds(b * 16 + n, 1)] * cb - sa[h, pl.ds(b * 16 + n, 1)] * sb
                table[pl.ds(base + n * 64, 64), d * R + h * 128:d * R + (h + 1) * 128] = value.astype(BF)

    def fold(j):
        low = slice(j * R, (j + 1) * R)
        high = slice(D - (j + 1) * R, D - j * R)
        lows = 0.9 * res[0, low] + gbuf[low].astype(F32)
        highs = 0.9 * res[0, high] + gbuf[high].astype(F32)
        res[0, low] = lows
        res[0, high] = highs
        turned = dot(mirror, highs.astype(BF))
        xt[0:CB, low] = dot_nt(unit, (lows + turned).astype(BF)).astype(BF)
        xt[CB:2 * CB, low] = dot_nt(unit, (lows - turned).astype(BF)).astype(BF)

    def split(d, both):
        lanes = slice(d * R, (d + 1) * R)
        odd = (frel[:, lanes] & 1) == 1
        own = jnp.where(odd, both[CB:], both[:CB]).astype(BF)
        coef[d] = own
        zero = jnp.zeros_like(own)
        seo[0:CB, lanes] = jnp.where(odd, zero, own)
        seo[CB:2 * CB, lanes] = jnp.where(odd, own, zero)

    def build_forward(d):
        waves = angles(d)
        acc[...] = jnp.zeros_like(acc)

        def step(b, carry):
            build(d, b, waves)
            rows = pl.ds(pl.multiple_of(b * 1024, 1024), 1024)
            acc[...] += dot(xt[:, rows], table[rows, d * R:(d + 1) * R])
            return carry

        lax.fori_loop(0, 4, step, 0)
        split(d, acc[...])

    M = 512

    def inverse(j, carry):
        total = dot_nt(table[pl.ds(pl.multiple_of(j * M, M), M)], seo[...])
        for n in range(M // R):
            low = pl.ds(pl.multiple_of(j * M, M) + n * R, R)
            high = pl.ds(pl.multiple_of(D - M - j * M, M) + (M - R - n * R), R)
            even, odd = total[n * R:(n + 1) * R, :CB], total[n * R:(n + 1) * R, CB:]
            res[0, low] -= even + odd
            res[0, high] -= dot(mirror, (even - odd).astype(BF))
        return carry

    def send_coef(d):
        send(CX + d - 1, coef.at[d], rsx.at[d - 1], xdev(d))

    waves = angles(2)

    def first(b, carry):
        build(2, b, waves)
        return carry

    lax.fori_loop(0, 4, first, 0)
    for s in range(4):
        for a, b in loads[2 * s:2 * s + 2]:
            a.wait()
            b.wait()
        for j in range(4 * s, 4 * s + 4):
            fold(j)
    split(2, dot(xt[...], table[:, 2 * R:3 * R]))
    send_coef(2)
    from_z(1, 7)
    build_forward(1)
    send_coef(1)
    arrived(TOK + 0, tok_half(y + 3, 0, T))
    send(TOK + 3, tok_half(y + 3, 0, T // 2), tok_half(y + 3, 0, T // 2), ydev(1))
    send(TOK + 5, tok_half(y + 3, 0, T), tok_half(y + 3, 0, T), twin)
    arrived(TOK + 1, tok_half(y + 1, 0, T))
    send(TOK + 4, tok_half(y + 1, T // 2, T // 2), tok_half(y + 1, T // 2, T // 2), ydev(3))
    send(TOK + 6, tok_half(y + 1, 0, T), tok_half(y + 1, 0, T), twin)
    build_forward(3)
    send_coef(3)
    from_z(2, 6)
    from_x(0)
    build_forward(0)

    total = coef[0].astype(F32)
    for d in range(1, X):
        arrived(CX + d - 1, rsx.at[d - 1])
        total += rsx[d - 1].astype(F32)
    rszs[...] = total.astype(BF).reshape(Z, 16, R)
    for d in (4, 3, 5, 2, 6, 1, 7):
        send(CZ + d - 1, rszs.at[(z + d) % Z], rszr.at[d - 1], zdev(d))
    from_z(3, 5, 4)
    from_x(1, 7)
    lax.fori_loop(0, 4, inverse, 0)
    part = rszs[z].astype(F32)
    for d in range(1, Z):
        arrived(CZ + d - 1, rszr.at[d - 1])
        part += rszr[d - 1].astype(F32)

    def s_rows(zz):
        return sbuf.at[0, pl.ds(pl.multiple_of((zz % Z) * 16, 16), 16)]

    sbuf[0, pl.ds(pl.multiple_of(z * 16, 16), 16)] = (part * (1.0 / REPLICAS)).astype(BF)
    for d in (4, 3, 5, 2, 6, 1, 7):
        send(GZ + d - 1, s_rows(z), s_rows(z), zdev(d))
    from_x(2, 6)
    arrived(TOK + 3, tok_half(y + 2, 0, T // 2))
    arrived(TOK + 4, tok_half(y + 2, T // 2, T // 2))
    send(TOK + 7, tok_half(y + 2, 0, T), tok_half(y + 2, 0, T), twin)
    lax.fori_loop(4, 8, inverse, 0)
    for d in range(1, Z):
        arrived(GZ + d - 1, s_rows(z - d + Z))
    for d in (2, 1, 3):
        send(GX + d - 1, sbuf.at[0], sbuf.at[X - d], xdev(d))
    from_x(3, 5, 4)

    arrived(TOK + 2, tok_twin(y))
    arrived(TOK + 5, tok_twin(y + 3))
    arrived(TOK + 6, tok_twin(y + 1))
    arrived(TOK + 7, tok_twin(y + 2))
    for j in range(H // R):
        b, o = j // 4, j % 4
        lows = tok[b, :, o * R:(o + 1) * R].astype(F32)
        turned = dot(tok[7 - b, :, (3 - o) * R:(4 - o) * R], mirror)
        tt[0:T, j * R:(j + 1) * R] = (lows + turned).astype(BF)
        tt[T:2 * T, j * R:(j + 1) * R] = (lows - turned).astype(BF)
    second = i >= REPLICAS // 2
    place = jnp.where(second, REPLICAS - 1 - i, i)
    pick = jnp.where(col == jnp.where(second, R - 1 - row, row), 1.0, 0.0).astype(BF)

    def token_step(d, carry):
        lanes = pl.ds(pl.multiple_of(d * R, R), R)
        both = dot(tt[...], table[:, lanes])
        odd = (frel[:, lanes] & 1) == 1
        left[pl.ds(R, T), lanes] = jnp.where(odd, both[T:], both[:T]).astype(BF)
        own = dot(pick, table[pl.ds(pl.multiple_of(place * R, R), R), lanes])
        left[pl.ds(0, R), lanes] = jnp.where(jnp.logical_and(odd, second), -own, own).astype(BF)
        return carry

    lax.fori_loop(0, X, token_step, 0)

    def plane(dx):
        xx = (x + dx) % X
        return (dot(tok[2 * xx], wbuf[xx, 0:4].reshape(1024, CB))
                + dot(tok[2 * xx + 1], wbuf[xx, 4:8].reshape(1024, CB)))

    found = plane(0) + plane(1) + plane(3)
    for n in range(4):
        arrived(FP + n, block(2, PASS_P[n]))
        arrived(FM + n, block(2, PASS_M[n]))
    found += plane(2)
    product = dot_nt(left[:, 0:R], sbuf[0])
    for d in range(1, X):
        arrived(GX + d - 1, sbuf.at[X - d])
        product += dot_nt(left[:, (X - d) * R:(X - d + 1) * R], sbuf[X - d])
    newm[...] = mbuf[...] - product[:R]
    keys[...] = ((found - product[R:]) * D ** -0.5).astype(BF)

    for copy in sent:
        copy.wait_send()


def store(res, newm, keys, res_out, newm_out, keys_out, sem):
    copies = [
        pltpu.make_async_copy(res, res_out, sem.at[0]),
        pltpu.make_async_copy(newm, newm_out, sem.at[1]),
        pltpu.make_async_copy(keys, keys_out, sem.at[2]),
    ]
    for copy in copies:
        copy.start()
    for copy in copies:
        copy.wait()


def body(momentum, gradient, masters, tokens, freq_index):
    hbm = pl.BlockSpec(memory_space=pl.ANY)
    vmem = pl.BlockSpec(memory_space=pltpu.VMEM)
    held = pl.pallas_call(
        kernel,
        out_shape=(
            pltpu.VMEM((1, D, CB), F32),
            pltpu.VMEM((R, CB), F32),
            pltpu.VMEM((T, CB), BF),
        ),
        in_specs=[hbm] * 5,
        out_specs=(vmem, vmem, vmem),
        scratch_shapes=[
            pltpu.VMEM((D, CB), BF),
            pltpu.VMEM((H, K), BF),
            pltpu.VMEM((2 * CB, H), BF),
            pltpu.VMEM((2 * CB, K), BF),
            pltpu.VMEM((X, CB, R), BF),
            pltpu.VMEM((X - 1, CB, R), BF),
            pltpu.VMEM((Z, 16, R), BF),
            pltpu.VMEM((Z - 1, 16, R), BF),
            pltpu.VMEM((X, CB, R), BF),
            pltpu.VMEM((8, T, 1024), BF),
            pltpu.VMEM((2 * T, H), BF),
            pltpu.VMEM((R + T, K), BF),
            pltpu.VMEM((X, Z, R, CB), BF),
            pltpu.VMEM((R, CB), F32),
            pltpu.VMEM((1, K), jnp.int32),
            pltpu.VMEM((1, K), jnp.int32),
            pltpu.VMEM((R, R), F32),
            pltpu.VMEM((2, 64, 128), F32),
            pltpu.VMEM((2, 64, 128), F32),
            pltpu.SemaphoreType.DMA((19,)),
            pltpu.SemaphoreType.DMA((MSGS,)),
            pltpu.SemaphoreType.DMA((MSGS,)),
        ],
        compiler_params=pltpu.CompilerParams(
            collective_id=0, has_side_effects=True, vmem_limit_bytes=56 * 1024 * 1024),
    )(momentum, gradient, masters, tokens, freq_index)
    return pl.pallas_call(
        store,
        out_shape=(
            jax.ShapeDtypeStruct((1, D, CB), F32),
            jax.ShapeDtypeStruct((R, CB), F32),
            jax.ShapeDtypeStruct((T, CB), BF),
        ),
        in_specs=[vmem] * 3,
        out_specs=(hbm, hbm, hbm),
        scratch_shapes=[pltpu.SemaphoreType.DMA((3,))],
        compiler_params=pltpu.CompilerParams(vmem_limit_bytes=4 * 1024 * 1024),
    )(*[pltpu.with_memory_space_constraint(a, pltpu.VMEM) for a in held])


def solution(mesh):
    return jax.shard_map(
        body,
        mesh=mesh,
        in_specs=(
            P("dp", None, "tensor"),
            P("dp", None, "tensor"),
            P("dp", "tensor"),
            P("dp", "tensor"),
            P("tensor", None),
        ),
        out_specs=(P("dp", None, "tensor"), P("dp", "tensor"), P("dp", "tensor")),
        check_vma=False,
    )
```

```python
import math

import jax
import jax.numpy as jnp
from jax import lax
from jax.experimental import pallas as pl
from jax.experimental.pallas import tpu as pltpu
from jax.sharding import PartitionSpec as P

D = 8192
H = D // 2
K = 1024
CB = 128
X, Z = 4, 8
REPLICAS = X * Z
R = 256
T = 128
BF = jnp.bfloat16
F32 = jnp.float32

TOK, MZ, XP, XM, FP, FM, CX, CZ, GZ, GX, MSGS = 0, 8, 15, 23, 31, 35, 39, 42, 49, 56, 59
PASS_P, PASS_M = (0, 1, 2, 3), (7, 6, 5, 4)


def dot(a, b):
    return jnp.dot(a, b, preferred_element_type=F32)


def dot_nt(a, b):
    return lax.dot_general(a, b, (((1,), (1,)), ((), ())), preferred_element_type=F32)


def cos_sin(phase):
    quadrant = (phase + 4096) >> 13
    angle = (phase - (quadrant << 13)).astype(F32) * (math.pi / 16384)
    square = angle * angle
    sine = angle * (1.0 + square * (-1 / 6 + square * (1 / 120 + square * (-1 / 5040))))
    cosine = 1.0 + square * (-0.5 + square * (1 / 24 + square * (-1 / 720 + square * (1 / 40320))))
    swap = (quadrant & 1) == 1
    c = jnp.where(swap, sine, cosine)
    s = jnp.where(swap, cosine, sine)
    c = jnp.where(((quadrant + 1) & 2) == 2, -c, c)
    s = jnp.where((quadrant & 2) == 2, -s, s)
    return c, s


def kernel(mom, grad, mast, tok_in, freq, res, newm, keys,
           gbuf, table, xt, seo, coef, rsx, rszs, rszr, sbuf, tok, tt, left, wbuf, mbuf, fbuf, frel, acc,
           ca, sa, ldsem, ssem, rsem):
    i = lax.axis_index("dp")
    t = lax.axis_index("tensor")
    x, z = i // Z, i % Z
    y, core = t // 2, t % 2

    def xdev(d):
        return (((x + d) % X) * Z + z, t)

    def zdev(d):
        return (x * Z + (z + d) % Z, t)

    def ydev(d):
        return (i, ((y + d) % 4) * 2 + core)

    twin = (i, y * 2 + (1 - core))

    barrier = pltpu.get_barrier_semaphore()
    peers = [xdev(d) for d in range(1, X)] + [zdev(d) for d in range(1, Z)] + [ydev(1), ydev(3), twin]
    for peer in peers:
        pl.semaphore_signal(barrier, inc=1, device_id=peer, device_id_type=pl.DeviceIdType.MESH)

    load_mast = pltpu.make_async_copy(mast, mbuf, ldsem.at[0])
    load_freq = pltpu.make_async_copy(freq, fbuf, ldsem.at[1])
    load_tok = pltpu.make_async_copy(tok_in, tok.at[t], ldsem.at[2])
    load_mast.start()
    load_tok.start()
    load_freq.start()
    loads = []
    for c in (0, 7, 1, 6, 2, 5, 3, 4):
        rows = pl.ds(1024 * c, 1024)
        a = pltpu.make_async_copy(mom.at[0, rows], res.at[0, rows], ldsem.at[3 + c])
        b = pltpu.make_async_copy(grad.at[0, rows], gbuf.at[rows], ldsem.at[11 + c])
        a.start()
        b.start()
        loads.append((a, b))

    sent = []

    def send(number, src, dst, device):
        copy = pltpu.make_async_remote_copy(
            src_ref=src, dst_ref=dst, send_sem=ssem.at[number], recv_sem=rsem.at[number],
            device_id=device, device_id_type=pl.DeviceIdType.MESH)
        copy.start()
        sent.append(copy)

    def arrived(number, ref):
        pltpu.make_async_remote_copy(
            src_ref=ref, dst_ref=ref, send_sem=ssem.at[number], recv_sem=rsem.at[number],
            device_id=twin, device_id_type=pl.DeviceIdType.MESH).wait_recv()

    load_mast.wait()
    wbuf[x, z] = mbuf[...].astype(BF)
    load_tok.wait()
    pl.semaphore_wait(barrier, len(peers))

    def block(dx, dz):
        return wbuf.at[(x + dx) % X, (z + dz) % Z]

    def spread(dz):
        send(XP + dz, block(0, dz), block(0, dz), xdev(1))
        send(XM + dz, block(0, dz), block(0, dz), xdev(3))

    def from_z(*offsets):
        for dz in offsets:
            arrived(MZ + (Z - dz) - 1, block(0, dz))
            spread(dz)

    def from_x(*offsets):
        for dz in offsets:
            arrived(XP + dz, block(3, dz))
            if dz in PASS_P:
                send(FP + PASS_P.index(dz), block(3, dz), block(3, dz), xdev(1))
            arrived(XM + dz, block(1, dz))
            if dz in PASS_M:
                send(FM + PASS_M.index(dz), block(1, dz), block(1, dz), xdev(3))

    def tok_half(yy, lo, n):
        return tok.at[(yy % 4) * 2 + core, pl.ds(lo, n)]

    def tok_twin(yy):
        return tok.at[(yy % 4) * 2 + 1 - core]

    send(TOK + 0, tok_half(y, 0, T), tok_half(y, 0, T), ydev(1))
    send(TOK + 1, tok_half(y, 0, T), tok_half(y, 0, T), ydev(3))
    for d in (1, 7, 2, 6):
        send(MZ + d - 1, block(0, 0), block(0, 0), zdev(d))
    spread(0)
    send(TOK + 2, tok_half(y, 0, T), tok_half(y, 0, T), twin)

    load_freq.wait()
    for d in range(X):
        frel[:, d * R:(d + 1) * R] = fbuf[:, pl.ds(pl.multiple_of(((x + d) % X) * R, R), R)]

    row = lax.broadcasted_iota(jnp.int32, (R, R), 0)
    col = lax.broadcasted_iota(jnp.int32, (R, R), 1)
    mirror = jnp.where(row + col == R - 1, 1.0, 0.0).astype(BF)
    unit = jnp.where(
        lax.broadcasted_iota(jnp.int32, (CB, CB), 0) == lax.broadcasted_iota(jnp.int32, (CB, CB), 1), 1.0, 0.0
    ).astype(BF)

    def angles(d):
        counts = lax.broadcasted_iota(jnp.int32, (64, 128), 0)
        waves = []
        for h in range(2):
            f = frel[:, d * R + h * 128:d * R + (h + 1) * 128]
            scale = jnp.where(f == 0, math.sqrt(1.0 / D), math.sqrt(2.0 / D)).astype(F32)
            c, s = cos_sin((counts * 128 * f) & 32767)
            ca[h] = c * scale
            sa[h] = s * scale
            waves.append(cos_sin(((2 * counts + 1) * f) & 32767))
        return waves

    def build(d, b, waves):
        base = pl.multiple_of(b * 1024, 1024)
        for n in range(16):
            for h in range(2):
                cb, sb = waves[h]
                value = ca[h, pl.ds(b * 16 + n, 1)] * cb - sa[h, pl.ds(b * 16 + n, 1)] * sb
                table[pl.ds(base + n * 64, 64), d * R + h * 128:d * R + (h + 1) * 128] = value.astype(BF)

    def fold(j):
        low = slice(j * R, (j + 1) * R)
        high = slice(D - (j + 1) * R, D - j * R)
        lows = 0.9 * res[0, low] + gbuf[low].astype(F32)
        highs = 0.9 * res[0, high] + gbuf[high].astype(F32)
        res[0, low] = lows
        res[0, high] = highs
        turned = dot(mirror, highs.astype(BF))
        xt[0:CB, low] = (lows + turned).astype(BF).T
        xt[CB:2 * CB, low] = (lows - turned).astype(BF).T

    def split(d, both):
        lanes = slice(d * R, (d + 1) * R)
        odd = (frel[:, lanes] & 1) == 1
        own = jnp.where(odd, both[CB:], both[:CB]).astype(BF)
        coef[d] = own
        zero = jnp.zeros_like(own)
        seo[0:CB, lanes] = jnp.where(odd, zero, own)
        seo[CB:2 * CB, lanes] = jnp.where(odd, own, zero)

    def build_forward(d):
        waves = angles(d)
        acc[...] = jnp.zeros_like(acc)

        def step(b, carry):
            build(d, b, waves)
            rows = pl.ds(pl.multiple_of(b * 1024, 1024), 1024)
            acc[...] += dot(xt[:, rows], table[rows, d * R:(d + 1) * R])
            return carry

        lax.fori_loop(0, 4, step, 0)
        split(d, acc[...])

    M = 1024

    def inverse(j, carry):
        total = dot_nt(table[pl.ds(pl.multiple_of(j * M, M), M)], seo[...])
        for n in range(M // R):
            low = pl.ds(pl.multiple_of(j * M, M) + n * R, R)
            high = pl.ds(pl.multiple_of(D - M - j * M, M) + (M - R - n * R), R)
            even, odd = total[n * R:(n + 1) * R, :CB], total[n * R:(n + 1) * R, CB:]
            res[0, low] -= even + odd
            res[0, high] -= dot(mirror, (even - odd).astype(BF))
        return carry

    def send_coef(d):
        send(CX + d - 1, coef.at[d], rsx.at[d - 1], xdev(d))

    waves = angles(2)

    def first(b, carry):
        build(2, b, waves)
        return carry

    lax.fori_loop(0, 4, first, 0)
    for s in range(4):
        for a, b in loads[2 * s:2 * s + 2]:
            a.wait()
            b.wait()
        for j in range(4 * s, 4 * s + 4):
            fold(j)
        if s == 1:
            for d in (3, 5, 4):
                send(MZ + d - 1, block(0, 0), block(0, 0), zdev(d))
    split(2, dot(xt[...], table[:, 2 * R:3 * R]))
    send_coef(2)
    from_z(1, 7)
    build_forward(1)
    send_coef(1)
    arrived(TOK + 0, tok_half(y + 3, 0, T))
    send(TOK + 3, tok_half(y + 3, 0, T // 2), tok_half(y + 3, 0, T // 2), ydev(1))
    send(TOK + 5, tok_half(y + 3, 0, T), tok_half(y + 3, 0, T), twin)
    arrived(TOK + 1, tok_half(y + 1, 0, T))
    send(TOK + 4, tok_half(y + 1, T // 2, T // 2), tok_half(y + 1, T // 2, T // 2), ydev(3))
    send(TOK + 6, tok_half(y + 1, 0, T), tok_half(y + 1, 0, T), twin)
    build_forward(3)
    send_coef(3)
    from_z(2, 6)
    build_forward(0)

    total = coef[0].astype(F32)
    for d in range(1, X):
        arrived(CX + d - 1, rsx.at[d - 1])
        total += rsx[d - 1].astype(F32)
    rszs[...] = total.astype(BF).reshape(Z, 16, R)
    for d in (4, 3, 5, 2, 6, 1, 7):
        send(CZ + d - 1, rszs.at[(z + d) % Z], rszr.at[d - 1], zdev(d))
    from_z(3, 5, 4)
    from_x(0)
    lax.fori_loop(0, 1, inverse, 0)
    from_x(1, 7)
    lax.fori_loop(1, 2, inverse, 0)
    part = rszs[z].astype(F32)
    for d in range(1, Z):
        arrived(CZ + d - 1, rszr.at[d - 1])
        part += rszr[d - 1].astype(F32)

    def s_rows(zz):
        return sbuf.at[0, pl.ds(pl.multiple_of((zz % Z) * 16, 16), 16)]

    sbuf[0, pl.ds(pl.multiple_of(z * 16, 16), 16)] = (part * (1.0 / REPLICAS)).astype(BF)
    for d in (4, 3, 5, 2, 6, 1, 7):
        send(GZ + d - 1, s_rows(z), s_rows(z), zdev(d))
    arrived(TOK + 3, tok_half(y + 2, 0, T // 2))
    arrived(TOK + 4, tok_half(y + 2, T // 2, T // 2))
    send(TOK + 7, tok_half(y + 2, 0, T), tok_half(y + 2, 0, T), twin)
    lax.fori_loop(2, 3, inverse, 0)
    from_x(2, 6)
    from_x(3, 5, 4)
    lax.fori_loop(3, 4, inverse, 0)
    for d in range(1, Z):
        arrived(GZ + d - 1, s_rows(z - d + Z))
    for d in (2, 1, 3):
        send(GX + d - 1, sbuf.at[0], sbuf.at[X - d], xdev(d))

    arrived(TOK + 2, tok_twin(y))
    arrived(TOK + 5, tok_twin(y + 3))
    arrived(TOK + 6, tok_twin(y + 1))
    arrived(TOK + 7, tok_twin(y + 2))
    for j in range(H // R):
        b, o = j // 4, j % 4
        lows = tok[b, :, o * R:(o + 1) * R].astype(F32)
        turned = dot(tok[7 - b, :, (3 - o) * R:(4 - o) * R], mirror)
        tt[0:T, j * R:(j + 1) * R] = (lows + turned).astype(BF)
        tt[T:2 * T, j * R:(j + 1) * R] = (lows - turned).astype(BF)
    second = i >= REPLICAS // 2
    place = jnp.where(second, REPLICAS - 1 - i, i)
    pick = jnp.where(col == jnp.where(second, R - 1 - row, row), 1.0, 0.0).astype(BF)

    def token_step(d, carry):
        lanes = pl.ds(pl.multiple_of(d * R, R), R)
        both = dot(tt[...], table[:, lanes])
        odd = (frel[:, lanes] & 1) == 1
        left[pl.ds(R, T), lanes] = jnp.where(odd, both[T:], both[:T]).astype(BF)
        own = dot(pick, table[pl.ds(pl.multiple_of(place * R, R), R), lanes])
        left[pl.ds(0, R), lanes] = jnp.where(jnp.logical_and(odd, second), -own, own).astype(BF)
        return carry

    lax.fori_loop(0, X, token_step, 0)

    def plane(dx):
        xx = (x + dx) % X
        return (dot(tok[2 * xx], wbuf[xx, 0:4].reshape(1024, CB))
                + dot(tok[2 * xx + 1], wbuf[xx, 4:8].reshape(1024, CB)))

    found = plane(0) + plane(1) + plane(3)
    for n in range(4):
        arrived(FP + n, block(2, PASS_P[n]))
        arrived(FM + n, block(2, PASS_M[n]))
    found += plane(2)
    product = dot_nt(left[:, 0:R], sbuf[0])
    for d in range(1, X):
        arrived(GX + d - 1, sbuf.at[X - d])
        product += dot_nt(left[:, (X - d) * R:(X - d + 1) * R], sbuf[X - d])
    newm[...] = mbuf[...] - product[:R]
    keys[...] = ((found - product[R:]) * D ** -0.5).astype(BF)

    for copy in sent:
        copy.wait_send()


def store(res, newm, keys, res_out, newm_out, keys_out, sem):
    copies = [
        pltpu.make_async_copy(res, res_out, sem.at[0]),
        pltpu.make_async_copy(newm, newm_out, sem.at[1]),
        pltpu.make_async_copy(keys, keys_out, sem.at[2]),
    ]
    for copy in copies:
        copy.start()
    for copy in copies:
        copy.wait()


def body(momentum, gradient, masters, tokens, freq_index):
    hbm = pl.BlockSpec(memory_space=pl.ANY)
    vmem = pl.BlockSpec(memory_space=pltpu.VMEM)
    held = pl.pallas_call(
        kernel,
        out_shape=(
            pltpu.VMEM((1, D, CB), F32),
            pltpu.VMEM((R, CB), F32),
            pltpu.VMEM((T, CB), BF),
        ),
        in_specs=[hbm] * 5,
        out_specs=(vmem, vmem, vmem),
        scratch_shapes=[
            pltpu.VMEM((D, CB), BF),
            pltpu.VMEM((H, K), BF),
            pltpu.VMEM((2 * CB, H), BF),
            pltpu.VMEM((2 * CB, K), BF),
            pltpu.VMEM((X, CB, R), BF),
            pltpu.VMEM((X - 1, CB, R), BF),
            pltpu.VMEM((Z, 16, R), BF),
            pltpu.VMEM((Z - 1, 16, R), BF),
            pltpu.VMEM((X, CB, R), BF),
            pltpu.VMEM((8, T, 1024), BF),
            pltpu.VMEM((2 * T, H), BF),
            pltpu.VMEM((R + T, K), BF),
            pltpu.VMEM((X, Z, R, CB), BF),
            pltpu.VMEM((R, CB), F32),
            pltpu.VMEM((1, K), jnp.int32),
            pltpu.VMEM((1, K), jnp.int32),
            pltpu.VMEM((R, R), F32),
            pltpu.VMEM((2, 64, 128), F32),
            pltpu.VMEM((2, 64, 128), F32),
            pltpu.SemaphoreType.DMA((19,)),
            pltpu.SemaphoreType.DMA((MSGS,)),
            pltpu.SemaphoreType.DMA((MSGS,)),
        ],
        compiler_params=pltpu.CompilerParams(
            collective_id=0, has_side_effects=True, vmem_limit_bytes=56 * 1024 * 1024),
    )(momentum, gradient, masters, tokens, freq_index)
    return pl.pallas_call(
        store,
        out_shape=(
            jax.ShapeDtypeStruct((1, D, CB), F32),
            jax.ShapeDtypeStruct((R, CB), F32),
            jax.ShapeDtypeStruct((T, CB), BF),
        ),
        in_specs=[vmem] * 3,
        out_specs=(hbm, hbm, hbm),
        scratch_shapes=[pltpu.SemaphoreType.DMA((3,))],
        compiler_params=pltpu.CompilerParams(vmem_limit_bytes=4 * 1024 * 1024),
    )(*[pltpu.with_memory_space_constraint(a, pltpu.VMEM) for a in held])


def solution(mesh):
    return jax.shard_map(
        body,
        mesh=mesh,
        in_specs=(
            P("dp", None, "tensor"),
            P("dp", None, "tensor"),
            P("dp", "tensor"),
            P("dp", "tensor"),
            P("tensor", None),
        ),
        out_specs=(P("dp", None, "tensor"), P("dp", "tensor"), P("dp", "tensor")),
        check_vma=False,
    )
```

```python
import math

import jax
import jax.numpy as jnp
from jax import lax
from jax.experimental import pallas as pl
from jax.experimental.pallas import tpu as pltpu
from jax.sharding import PartitionSpec as P

D = 8192
H = D // 2
K = 1024
CB = 128
X, Z = 4, 8
REPLICAS = X * Z
R = 256
T = 128
BF = jnp.bfloat16
F32 = jnp.float32

TOK, MZ, XP, XM, FP, FM, CX, CZ, GZ, GX, MSGS = 0, 8, 15, 23, 31, 35, 39, 42, 49, 56, 59
PASS_P, PASS_M = (0, 1, 2, 3), (7, 6, 5, 4)


def dot(a, b):
    return jnp.dot(a, b, preferred_element_type=F32)


def dot_nt(a, b):
    return lax.dot_general(a, b, (((1,), (1,)), ((), ())), preferred_element_type=F32)


def cos_sin(phase):
    quadrant = (phase + 4096) >> 13
    angle = (phase - (quadrant << 13)).astype(F32) * (math.pi / 16384)
    square = angle * angle
    sine = angle * (1.0 + square * (-1 / 6 + square * (1 / 120 + square * (-1 / 5040))))
    cosine = 1.0 + square * (-0.5 + square * (1 / 24 + square * (-1 / 720 + square * (1 / 40320))))
    swap = (quadrant & 1) == 1
    c = jnp.where(swap, sine, cosine)
    s = jnp.where(swap, cosine, sine)
    c = jnp.where(((quadrant + 1) & 2) == 2, -c, c)
    s = jnp.where((quadrant & 2) == 2, -s, s)
    return c, s


def kernel(mom, grad, mast, tok_in, freq, res, newm, keys,
           gbuf, table, xt, seo, coef, rsx, rszs, rszr, sbuf, tok, tt, left, wbuf, mbuf, fbuf, frel, acc,
           ca, sa, ldsem, ssem, rsem):
    i = lax.axis_index("dp")
    t = lax.axis_index("tensor")
    x, z = i // Z, i % Z
    y, core = t // 2, t % 2

    def xdev(d):
        return (((x + d) % X) * Z + z, t)

    def zdev(d):
        return (x * Z + (z + d) % Z, t)

    def ydev(d):
        return (i, ((y + d) % 4) * 2 + core)

    twin = (i, y * 2 + (1 - core))

    barrier = pltpu.get_barrier_semaphore()
    peers = [xdev(d) for d in range(1, X)] + [zdev(d) for d in range(1, Z)] + [ydev(1), ydev(3), twin]
    for peer in peers:
        pl.semaphore_signal(barrier, inc=1, device_id=peer, device_id_type=pl.DeviceIdType.MESH)

    load_mast = pltpu.make_async_copy(mast, mbuf, ldsem.at[0])
    load_freq = pltpu.make_async_copy(freq, fbuf, ldsem.at[1])
    load_tok = pltpu.make_async_copy(tok_in, tok.at[t], ldsem.at[2])
    load_mast.start()
    load_tok.start()
    load_freq.start()
    loads = []
    for c in (0, 7, 1, 6, 2, 5, 3, 4):
        rows = pl.ds(1024 * c, 1024)
        a = pltpu.make_async_copy(mom.at[0, rows], res.at[0, rows], ldsem.at[3 + c])
        b = pltpu.make_async_copy(grad.at[0, rows], gbuf.at[rows], ldsem.at[11 + c])
        a.start()
        b.start()
        loads.append((a, b))

    sent = []

    def send(number, src, dst, device):
        copy = pltpu.make_async_remote_copy(
            src_ref=src, dst_ref=dst, send_sem=ssem.at[number], recv_sem=rsem.at[number],
            device_id=device, device_id_type=pl.DeviceIdType.MESH)
        copy.start()
        sent.append(copy)

    def arrived(number, ref):
        pltpu.make_async_remote_copy(
            src_ref=ref, dst_ref=ref, send_sem=ssem.at[number], recv_sem=rsem.at[number],
            device_id=twin, device_id_type=pl.DeviceIdType.MESH).wait_recv()

    load_mast.wait()
    wbuf[x, z] = mbuf[...].astype(BF)
    load_tok.wait()
    pl.semaphore_wait(barrier, len(peers))

    def block(dx, dz):
        return wbuf.at[(x + dx) % X, (z + dz) % Z]

    def spread(dz):
        send(XP + dz, block(0, dz), block(0, dz), xdev(1))
        send(XM + dz, block(0, dz), block(0, dz), xdev(3))

    def from_z(*offsets):
        for dz in offsets:
            arrived(MZ + (Z - dz) - 1, block(0, dz))
            if dz == 6:
                send(MZ + 2, block(0, 6), block(0, 6), zdev(1))
                send(MZ + 3, block(0, 6), block(0, 6), zdev(2))
            if dz == 2:
                send(MZ + 4, block(0, 2), block(0, 2), zdev(Z - 1))
            spread(dz)

    def from_x(*offsets):
        for dz in offsets:
            arrived(XP + dz, block(3, dz))
            if dz in PASS_P:
                send(FP + PASS_P.index(dz), block(3, dz), block(3, dz), xdev(1))
            arrived(XM + dz, block(1, dz))
            if dz in PASS_M:
                send(FM + PASS_M.index(dz), block(1, dz), block(1, dz), xdev(3))

    def tok_half(yy, lo, n):
        return tok.at[(yy % 4) * 2 + core, pl.ds(lo, n)]

    def tok_twin(yy):
        return tok.at[(yy % 4) * 2 + 1 - core]

    send(TOK + 0, tok_half(y, 0, T), tok_half(y, 0, T), ydev(1))
    send(TOK + 1, tok_half(y, 0, T), tok_half(y, 0, T), ydev(3))
    for d in (1, 7, 2, 6):
        send(MZ + d - 1, block(0, 0), block(0, 0), zdev(d))
    spread(0)
    send(TOK + 2, tok_half(y, 0, T), tok_half(y, 0, T), twin)

    load_freq.wait()
    for d in range(X):
        frel[:, d * R:(d + 1) * R] = fbuf[:, pl.ds(pl.multiple_of(((x + d) % X) * R, R), R)]

    row = lax.broadcasted_iota(jnp.int32, (R, R), 0)
    col = lax.broadcasted_iota(jnp.int32, (R, R), 1)
    mirror = jnp.where(row + col == R - 1, 1.0, 0.0).astype(BF)
    unit = jnp.where(
        lax.broadcasted_iota(jnp.int32, (CB, CB), 0) == lax.broadcasted_iota(jnp.int32, (CB, CB), 1), 1.0, 0.0
    ).astype(BF)

    def angles(d):
        counts = lax.broadcasted_iota(jnp.int32, (64, 128), 0)
        waves = []
        for h in range(2):
            f = frel[:, d * R + h * 128:d * R + (h + 1) * 128]
            scale = jnp.where(f == 0, math.sqrt(1.0 / D), math.sqrt(2.0 / D)).astype(F32)
            c, s = cos_sin((counts * 128 * f) & 32767)
            ca[h] = c * scale
            sa[h] = s * scale
            waves.append(cos_sin(((2 * counts + 1) * f) & 32767))
        return waves

    def build(d, b, waves):
        base = pl.multiple_of(b * 1024, 1024)
        for n in range(16):
            for h in range(2):
                cb, sb = waves[h]
                value = ca[h, pl.ds(b * 16 + n, 1)] * cb - sa[h, pl.ds(b * 16 + n, 1)] * sb
                table[pl.ds(base + n * 64, 64), d * R + h * 128:d * R + (h + 1) * 128] = value.astype(BF)

    def fold(j):
        low = slice(j * R, (j + 1) * R)
        high = slice(D - (j + 1) * R, D - j * R)
        lows = 0.9 * res[0, low] + gbuf[low].astype(F32)
        highs = 0.9 * res[0, high] + gbuf[high].astype(F32)
        res[0, low] = lows
        res[0, high] = highs
        turned = dot(mirror, highs.astype(BF))
        xt[0:CB, low] = (lows + turned).astype(BF).T
        xt[CB:2 * CB, low] = (lows - turned).astype(BF).T

    def split(d, both):
        lanes = slice(d * R, (d + 1) * R)
        odd = (frel[:, lanes] & 1) == 1
        own = jnp.where(odd, both[CB:], both[:CB]).astype(BF)
        coef[d] = own
        zero = jnp.zeros_like(own)
        seo[0:CB, lanes] = jnp.where(odd, zero, own)
        seo[CB:2 * CB, lanes] = jnp.where(odd, own, zero)

    def build_forward(d):
        waves = angles(d)
        acc[...] = jnp.zeros_like(acc)

        def step(b, carry):
            build(d, b, waves)
            rows = pl.ds(pl.multiple_of(b * 1024, 1024), 1024)
            acc[...] += dot(xt[:, rows], table[rows, d * R:(d + 1) * R])
            return carry

        lax.fori_loop(0, 4, step, 0)
        split(d, acc[...])

    M = 1024

    def inverse(j, carry):
        total = dot_nt(table[pl.ds(pl.multiple_of(j * M, M), M)], seo[...])
        for n in range(M // R):
            low = pl.ds(pl.multiple_of(j * M, M) + n * R, R)
            high = pl.ds(pl.multiple_of(D - M - j * M, M) + (M - R - n * R), R)
            even, odd = total[n * R:(n + 1) * R, :CB], total[n * R:(n + 1) * R, CB:]
            res[0, low] -= even + odd
            res[0, high] -= dot(mirror, (even - odd).astype(BF))
        return carry

    def send_coef(d):
        send(CX + d - 1, coef.at[d], rsx.at[d - 1], xdev(d))

    waves = angles(2)

    def first(b, carry):
        build(2, b, waves)
        return carry

    lax.fori_loop(0, 4, first, 0)
    for s in range(4):
        for a, b in loads[2 * s:2 * s + 2]:
            a.wait()
            b.wait()
        for j in range(4 * s, 4 * s + 4):
            fold(j)
    split(2, dot(xt[...], table[:, 2 * R:3 * R]))
    send_coef(2)
    from_z(1, 7)
    build_forward(1)
    send_coef(1)
    arrived(TOK + 0, tok_half(y + 3, 0, T))
    send(TOK + 3, tok_half(y + 3, 0, T // 2), tok_half(y + 3, 0, T // 2), ydev(1))
    send(TOK + 5, tok_half(y + 3, 0, T), tok_half(y + 3, 0, T), twin)
    arrived(TOK + 1, tok_half(y + 1, 0, T))
    send(TOK + 4, tok_half(y + 1, T // 2, T // 2), tok_half(y + 1, T // 2, T // 2), ydev(3))
    send(TOK + 6, tok_half(y + 1, 0, T), tok_half(y + 1, 0, T), twin)
    from_z(2, 6)
    build_forward(3)
    send_coef(3)
    from_x(0)
    build_forward(0)

    total = coef[0].astype(F32)
    for d in range(1, X):
        arrived(CX + d - 1, rsx.at[d - 1])
        total += rsx[d - 1].astype(F32)
    rszs[...] = total.astype(BF).reshape(Z, 16, R)
    for d in (4, 3, 5, 2, 6, 1, 7):
        send(CZ + d - 1, rszs.at[(z + d) % Z], rszr.at[d - 1], zdev(d))
    from_z(3, 5, 4)
    lax.fori_loop(0, 1, inverse, 0)
    from_x(1, 7)
    lax.fori_loop(1, 2, inverse, 0)
    part = rszs[z].astype(F32)
    for d in range(1, Z):
        arrived(CZ + d - 1, rszr.at[d - 1])
        part += rszr[d - 1].astype(F32)

    def s_rows(zz):
        return sbuf.at[0, pl.ds(pl.multiple_of((zz % Z) * 16, 16), 16)]

    sbuf[0, pl.ds(pl.multiple_of(z * 16, 16), 16)] = (part * (1.0 / REPLICAS)).astype(BF)
    for d in (4, 3, 5, 2, 6, 1, 7):
        send(GZ + d - 1, s_rows(z), s_rows(z), zdev(d))
    arrived(TOK + 3, tok_half(y + 2, 0, T // 2))
    arrived(TOK + 4, tok_half(y + 2, T // 2, T // 2))
    send(TOK + 7, tok_half(y + 2, 0, T), tok_half(y + 2, 0, T), twin)
    lax.fori_loop(2, 3, inverse, 0)
    from_x(2, 6)
    from_x(3, 5, 4)
    lax.fori_loop(3, 4, inverse, 0)
    for d in range(1, Z):
        arrived(GZ + d - 1, s_rows(z - d + Z))
    for d in (2, 1, 3):
        send(GX + d - 1, sbuf.at[0], sbuf.at[X - d], xdev(d))

    arrived(TOK + 2, tok_twin(y))
    arrived(TOK + 5, tok_twin(y + 3))
    arrived(TOK + 6, tok_twin(y + 1))
    arrived(TOK + 7, tok_twin(y + 2))
    for j in range(H // R):
        b, o = j // 4, j % 4
        lows = tok[b, :, o * R:(o + 1) * R].astype(F32)
        turned = dot(tok[7 - b, :, (3 - o) * R:(4 - o) * R], mirror)
        tt[0:T, j * R:(j + 1) * R] = (lows + turned).astype(BF)
        tt[T:2 * T, j * R:(j + 1) * R] = (lows - turned).astype(BF)
    second = i >= REPLICAS // 2
    place = jnp.where(second, REPLICAS - 1 - i, i)
    pick = jnp.where(col == jnp.where(second, R - 1 - row, row), 1.0, 0.0).astype(BF)

    def token_step(d, carry):
        lanes = pl.ds(pl.multiple_of(d * R, R), R)
        both = dot(tt[...], table[:, lanes])
        odd = (frel[:, lanes] & 1) == 1
        left[pl.ds(R, T), lanes] = jnp.where(odd, both[T:], both[:T]).astype(BF)
        own = dot(pick, table[pl.ds(pl.multiple_of(place * R, R), R), lanes])
        left[pl.ds(0, R), lanes] = jnp.where(jnp.logical_and(odd, second), -own, own).astype(BF)
        return carry

    lax.fori_loop(0, X, token_step, 0)

    def plane(dx):
        xx = (x + dx) % X
        return (dot(tok[2 * xx], wbuf[xx, 0:4].reshape(1024, CB))
                + dot(tok[2 * xx + 1], wbuf[xx, 4:8].reshape(1024, CB)))

    found = plane(0) + plane(1) + plane(3)
    for n in range(4):
        arrived(FP + n, block(2, PASS_P[n]))
        arrived(FM + n, block(2, PASS_M[n]))
    found += plane(2)
    product = dot_nt(left[:, 0:R], sbuf[0])
    for d in range(1, X):
        arrived(GX + d - 1, sbuf.at[X - d])
        product += dot_nt(left[:, (X - d) * R:(X - d + 1) * R], sbuf[X - d])
    newm[...] = mbuf[...] - product[:R]
    keys[...] = ((found - product[R:]) * D ** -0.5).astype(BF)

    for copy in sent:
        copy.wait_send()


def store(res, newm, keys, res_out, newm_out, keys_out, sem):
    copies = [
        pltpu.make_async_copy(res, res_out, sem.at[0]),
        pltpu.make_async_copy(newm, newm_out, sem.at[1]),
        pltpu.make_async_copy(keys, keys_out, sem.at[2]),
    ]
    for copy in copies:
        copy.start()
    for copy in copies:
        copy.wait()


def body(momentum, gradient, masters, tokens, freq_index):
    hbm = pl.BlockSpec(memory_space=pl.ANY)
    vmem = pl.BlockSpec(memory_space=pltpu.VMEM)
    held = pl.pallas_call(
        kernel,
        out_shape=(
            pltpu.VMEM((1, D, CB), F32),
            pltpu.VMEM((R, CB), F32),
            pltpu.VMEM((T, CB), BF),
        ),
        in_specs=[hbm] * 5,
        out_specs=(vmem, vmem, vmem),
        scratch_shapes=[
            pltpu.VMEM((D, CB), BF),
            pltpu.VMEM((H, K), BF),
            pltpu.VMEM((2 * CB, H), BF),
            pltpu.VMEM((2 * CB, K), BF),
            pltpu.VMEM((X, CB, R), BF),
            pltpu.VMEM((X - 1, CB, R), BF),
            pltpu.VMEM((Z, 16, R), BF),
            pltpu.VMEM((Z - 1, 16, R), BF),
            pltpu.VMEM((X, CB, R), BF),
            pltpu.VMEM((8, T, 1024), BF),
            pltpu.VMEM((2 * T, H), BF),
            pltpu.VMEM((R + T, K), BF),
            pltpu.VMEM((X, Z, R, CB), BF),
            pltpu.VMEM((R, CB), F32),
            pltpu.VMEM((1, K), jnp.int32),
            pltpu.VMEM((1, K), jnp.int32),
            pltpu.VMEM((R, R), F32),
            pltpu.VMEM((2, 64, 128), F32),
            pltpu.VMEM((2, 64, 128), F32),
            pltpu.SemaphoreType.DMA((19,)),
            pltpu.SemaphoreType.DMA((MSGS,)),
            pltpu.SemaphoreType.DMA((MSGS,)),
        ],
        compiler_params=pltpu.CompilerParams(
            collective_id=0, has_side_effects=True, vmem_limit_bytes=56 * 1024 * 1024),
    )(momentum, gradient, masters, tokens, freq_index)
    return pl.pallas_call(
        store,
        out_shape=(
            jax.ShapeDtypeStruct((1, D, CB), F32),
            jax.ShapeDtypeStruct((R, CB), F32),
            jax.ShapeDtypeStruct((T, CB), BF),
        ),
        in_specs=[vmem] * 3,
        out_specs=(hbm, hbm, hbm),
        scratch_shapes=[pltpu.SemaphoreType.DMA((3,))],
        compiler_params=pltpu.CompilerParams(vmem_limit_bytes=4 * 1024 * 1024),
    )(*[pltpu.with_memory_space_constraint(a, pltpu.VMEM) for a in held])


def solution(mesh):
    return jax.shard_map(
        body,
        mesh=mesh,
        in_specs=(
            P("dp", None, "tensor"),
            P("dp", None, "tensor"),
            P("dp", "tensor"),
            P("dp", "tensor"),
            P("tensor", None),
        ),
        out_specs=(P("dp", None, "tensor"), P("dp", "tensor"), P("dp", "tensor")),
        check_vma=False,
    )
```

```python
import math

import jax
import jax.numpy as jnp
from jax import lax
from jax.experimental import pallas as pl
from jax.experimental.pallas import tpu as pltpu
from jax.sharding import PartitionSpec as P

D = 8192
H = D // 2
K = 1024
CB = 128
X, Z = 4, 8
REPLICAS = X * Z
R = 256
T = 128
BF = jnp.bfloat16
F32 = jnp.float32

TOK, MZ, XP, XM, FP, FM, CX, CZ, GZ, GX, MSGS = 0, 8, 15, 23, 31, 35, 39, 42, 49, 56, 59
PASS_P, PASS_M = (0, 1, 2, 3), (7, 6, 5, 4)


def dot(a, b):
    return jnp.dot(a, b, preferred_element_type=F32)


def dot_nt(a, b):
    return lax.dot_general(a, b, (((1,), (1,)), ((), ())), preferred_element_type=F32)


def cos_sin(phase):
    quadrant = (phase + 4096) >> 13
    angle = (phase - (quadrant << 13)).astype(F32) * (math.pi / 16384)
    square = angle * angle
    sine = angle * (1.0 + square * (-1 / 6 + square * (1 / 120 + square * (-1 / 5040))))
    cosine = 1.0 + square * (-0.5 + square * (1 / 24 + square * (-1 / 720 + square * (1 / 40320))))
    swap = (quadrant & 1) == 1
    c = jnp.where(swap, sine, cosine)
    s = jnp.where(swap, cosine, sine)
    c = jnp.where(((quadrant + 1) & 2) == 2, -c, c)
    s = jnp.where((quadrant & 2) == 2, -s, s)
    return c, s


def kernel(mom, grad, mast, tok_in, freq, res, newm, keys,
           gbuf, table, xt, seo, coef, rsx, rszs, rszr, sbuf, tok, tt, left, wbuf, mbuf, fbuf, frel, acc,
           ca, sa, ldsem, ssem, rsem):
    i = lax.axis_index("dp")
    t = lax.axis_index("tensor")
    x, z = i // Z, i % Z
    y, core = t // 2, t % 2

    def xdev(d):
        return (((x + d) % X) * Z + z, t)

    def zdev(d):
        return (x * Z + (z + d) % Z, t)

    def ydev(d):
        return (i, ((y + d) % 4) * 2 + core)

    twin = (i, y * 2 + (1 - core))

    barrier = pltpu.get_barrier_semaphore()
    peers = [xdev(d) for d in range(1, X)] + [zdev(d) for d in range(1, Z)] + [ydev(1), ydev(3), twin]
    for peer in peers:
        pl.semaphore_signal(barrier, inc=1, device_id=peer, device_id_type=pl.DeviceIdType.MESH)

    load_mast = pltpu.make_async_copy(mast, mbuf, ldsem.at[0])
    load_freq = pltpu.make_async_copy(freq, fbuf, ldsem.at[1])
    load_tok = pltpu.make_async_copy(tok_in, tok.at[t], ldsem.at[2])
    load_mast.start()
    load_tok.start()
    load_freq.start()
    loads = []
    for c in (0, 7, 1, 6, 2, 5, 3, 4):
        rows = pl.ds(1024 * c, 1024)
        a = pltpu.make_async_copy(mom.at[0, rows], res.at[0, rows], ldsem.at[3 + c])
        b = pltpu.make_async_copy(grad.at[0, rows], gbuf.at[rows], ldsem.at[11 + c])
        a.start()
        b.start()
        loads.append((a, b))

    sent = []

    def send(number, src, dst, device):
        copy = pltpu.make_async_remote_copy(
            src_ref=src, dst_ref=dst, send_sem=ssem.at[number], recv_sem=rsem.at[number],
            device_id=device, device_id_type=pl.DeviceIdType.MESH)
        copy.start()
        sent.append(copy)

    def arrived(number, ref):
        pltpu.make_async_remote_copy(
            src_ref=ref, dst_ref=ref, send_sem=ssem.at[number], recv_sem=rsem.at[number],
            device_id=twin, device_id_type=pl.DeviceIdType.MESH).wait_recv()

    load_mast.wait()
    wbuf[x, z] = mbuf[...].astype(BF)
    load_tok.wait()
    pl.semaphore_wait(barrier, len(peers))

    def block(dx, dz):
        return wbuf.at[(x + dx) % X, (z + dz) % Z]

    def spread(dz):
        send(XP + dz, block(0, dz), block(0, dz), xdev(1))
        send(XM + dz, block(0, dz), block(0, dz), xdev(3))

    def from_z(*offsets):
        for dz in offsets:
            arrived(MZ + (Z - dz) - 1, block(0, dz))
            if dz == 6:
                send(MZ + 2, block(0, 6), block(0, 6), zdev(1))
                send(MZ + 3, block(0, 6), block(0, 6), zdev(2))
            if dz == 2:
                send(MZ + 4, block(0, 2), block(0, 2), zdev(Z - 1))
            spread(dz)

    def from_x(*offsets):
        for dz in offsets:
            arrived(XP + dz, block(3, dz))
            if dz in PASS_P:
                send(FP + PASS_P.index(dz), block(3, dz), block(3, dz), xdev(1))
            arrived(XM + dz, block(1, dz))
            if dz in PASS_M:
                send(FM + PASS_M.index(dz), block(1, dz), block(1, dz), xdev(3))

    def tok_half(yy, lo, n):
        return tok.at[(yy % 4) * 2 + core, pl.ds(lo, n)]

    def tok_twin(yy):
        return tok.at[(yy % 4) * 2 + 1 - core]

    send(TOK + 0, tok_half(y, 0, T), tok_half(y, 0, T), ydev(1))
    send(TOK + 1, tok_half(y, 0, T), tok_half(y, 0, T), ydev(3))
    for d in (1, 7, 2, 6):
        send(MZ + d - 1, block(0, 0), block(0, 0), zdev(d))
    spread(0)
    send(TOK + 2, tok_half(y, 0, T), tok_half(y, 0, T), twin)

    load_freq.wait()
    for d in range(X):
        frel[:, d * R:(d + 1) * R] = fbuf[:, pl.ds(pl.multiple_of(((x + d) % X) * R, R), R)]

    row = lax.broadcasted_iota(jnp.int32, (R, R), 0)
    col = lax.broadcasted_iota(jnp.int32, (R, R), 1)
    mirror = jnp.where(row + col == R - 1, 1.0, 0.0).astype(BF)
    unit = jnp.where(
        lax.broadcasted_iota(jnp.int32, (CB, CB), 0) == lax.broadcasted_iota(jnp.int32, (CB, CB), 1), 1.0, 0.0
    ).astype(BF)

    def angles(d):
        counts = lax.broadcasted_iota(jnp.int32, (64, 128), 0)
        waves = []
        for h in range(2):
            f = frel[:, d * R + h * 128:d * R + (h + 1) * 128]
            scale = jnp.where(f == 0, math.sqrt(1.0 / D), math.sqrt(2.0 / D)).astype(F32)
            c, s = cos_sin((counts * 128 * f) & 32767)
            ca[h] = c * scale
            sa[h] = s * scale
            waves.append(cos_sin(((2 * counts + 1) * f) & 32767))
        return waves

    def build(d, b, waves):
        base = pl.multiple_of(b * 1024, 1024)
        for n in range(16):
            for h in range(2):
                cb, sb = waves[h]
                value = ca[h, pl.ds(b * 16 + n, 1)] * cb - sa[h, pl.ds(b * 16 + n, 1)] * sb
                table[pl.ds(base + n * 64, 64), d * R + h * 128:d * R + (h + 1) * 128] = value.astype(BF)

    def fold(j):
        low = slice(j * R, (j + 1) * R)
        high = slice(D - (j + 1) * R, D - j * R)
        lows = 0.9 * res[0, low] + gbuf[low].astype(F32)
        highs = 0.9 * res[0, high] + gbuf[high].astype(F32)
        res[0, low] = lows
        res[0, high] = highs
        turned = dot(mirror, highs.astype(BF))
        xt[0:CB, low] = (lows + turned).astype(BF).T
        xt[CB:2 * CB, low] = (lows - turned).astype(BF).T

    def split(d, both):
        lanes = slice(d * R, (d + 1) * R)
        odd = (frel[:, lanes] & 1) == 1
        own = jnp.where(odd, both[CB:], both[:CB]).astype(BF)
        coef[d] = own
        zero = jnp.zeros_like(own)
        seo[0:CB, lanes] = jnp.where(odd, zero, own)
        seo[CB:2 * CB, lanes] = jnp.where(odd, own, zero)

    def build_forward(d):
        waves = angles(d)
        acc[...] = jnp.zeros_like(acc)

        def step(b, carry):
            build(d, b, waves)
            rows = pl.ds(pl.multiple_of(b * 1024, 1024), 1024)
            acc[...] += dot(xt[:, rows], table[rows, d * R:(d + 1) * R])
            return carry

        lax.fori_loop(0, 4, step, 0)
        split(d, acc[...])

    M = 1024

    def inverse(j, carry):
        total = dot_nt(table[pl.ds(pl.multiple_of(j * M, M), M)], seo[...])
        for n in range(M // R):
            low = pl.ds(pl.multiple_of(j * M, M) + n * R, R)
            high = pl.ds(pl.multiple_of(D - M - j * M, M) + (M - R - n * R), R)
            even, odd = total[n * R:(n + 1) * R, :CB], total[n * R:(n + 1) * R, CB:]
            res[0, low] -= even + odd
            res[0, high] -= dot(mirror, (even - odd).astype(BF))
        return carry

    def send_coef(d):
        send(CX + d - 1, coef.at[d], rsx.at[d - 1], xdev(d))

    waves = angles(2)

    def first(b, carry):
        build(2, b, waves)
        return carry

    lax.fori_loop(0, 4, first, 0)
    for s in range(4):
        for a, b in loads[2 * s:2 * s + 2]:
            a.wait()
            b.wait()
        for j in range(4 * s, 4 * s + 4):
            fold(j)
    split(2, dot(xt[...], table[:, 2 * R:3 * R]))
    send_coef(2)
    from_z(1, 7)
    build_forward(1)
    send_coef(1)
    arrived(TOK + 0, tok_half(y + 3, 0, T))
    send(TOK + 3, tok_half(y + 3, 0, T // 2), tok_half(y + 3, 0, T // 2), ydev(1))
    send(TOK + 5, tok_half(y + 3, 0, T), tok_half(y + 3, 0, T), twin)
    arrived(TOK + 1, tok_half(y + 1, 0, T))
    send(TOK + 4, tok_half(y + 1, T // 2, T // 2), tok_half(y + 1, T // 2, T // 2), ydev(3))
    send(TOK + 6, tok_half(y + 1, 0, T), tok_half(y + 1, 0, T), twin)
    from_z(2, 6)
    build_forward(3)
    send_coef(3)
    from_x(0)
    build_forward(0)

    total = coef[0].astype(F32)
    for d in range(1, X):
        arrived(CX + d - 1, rsx.at[d - 1])
        total += rsx[d - 1].astype(F32)
    rszs[...] = total.astype(BF).reshape(Z, 16, R)
    for d in (4, 3, 5, 2, 6, 1, 7):
        send(CZ + d - 1, rszs.at[(z + d) % Z], rszr.at[d - 1], zdev(d))
    from_z(3, 5, 4)
    lax.fori_loop(0, 1, inverse, 0)
    from_x(1, 7)
    lax.fori_loop(1, 2, inverse, 0)
    part = rszs[z].astype(F32)
    for d in range(1, Z):
        arrived(CZ + d - 1, rszr.at[d - 1])
        part += rszr[d - 1].astype(F32)

    def s_rows(zz):
        return sbuf.at[0, pl.ds(pl.multiple_of((zz % Z) * 16, 16), 16)]

    sbuf[0, pl.ds(pl.multiple_of(z * 16, 16), 16)] = (part * (1.0 / REPLICAS)).astype(BF)
    for d in (4, 3, 5, 2, 6, 1, 7):
        send(GZ + d - 1, s_rows(z), s_rows(z), zdev(d))
    arrived(TOK + 3, tok_half(y + 2, 0, T // 2))
    arrived(TOK + 4, tok_half(y + 2, T // 2, T // 2))
    send(TOK + 7, tok_half(y + 2, 0, T), tok_half(y + 2, 0, T), twin)
    lax.fori_loop(2, 3, inverse, 0)
    from_x(2, 6)
    lax.fori_loop(3, 4, inverse, 0)
    for d in range(1, Z):
        arrived(GZ + d - 1, s_rows(z - d + Z))
    for d in (2, 1, 3):
        send(GX + d - 1, sbuf.at[0], sbuf.at[X - d], xdev(d))
    from_x(3, 5, 4)

    arrived(TOK + 2, tok_twin(y))
    arrived(TOK + 5, tok_twin(y + 3))
    arrived(TOK + 6, tok_twin(y + 1))
    arrived(TOK + 7, tok_twin(y + 2))
    for j in range(H // R):
        b, o = j // 4, j % 4
        lows = tok[b, :, o * R:(o + 1) * R].astype(F32)
        turned = dot(tok[7 - b, :, (3 - o) * R:(4 - o) * R], mirror)
        tt[0:T, j * R:(j + 1) * R] = (lows + turned).astype(BF)
        tt[T:2 * T, j * R:(j + 1) * R] = (lows - turned).astype(BF)
    second = i >= REPLICAS // 2
    place = jnp.where(second, REPLICAS - 1 - i, i)
    pick = jnp.where(col == jnp.where(second, R - 1 - row, row), 1.0, 0.0).astype(BF)

    def token_step(d, carry):
        lanes = pl.ds(pl.multiple_of(d * R, R), R)
        both = dot(tt[...], table[:, lanes])
        odd = (frel[:, lanes] & 1) == 1
        left[pl.ds(R, T), lanes] = jnp.where(odd, both[T:], both[:T]).astype(BF)
        own = dot(pick, table[pl.ds(pl.multiple_of(place * R, R), R), lanes])
        left[pl.ds(0, R), lanes] = jnp.where(jnp.logical_and(odd, second), -own, own).astype(BF)
        return carry

    lax.fori_loop(0, X, token_step, 0)

    def plane(dx):
        xx = (x + dx) % X
        return (dot(tok[2 * xx], wbuf[xx, 0:4].reshape(1024, CB))
                + dot(tok[2 * xx + 1], wbuf[xx, 4:8].reshape(1024, CB)))

    found = plane(0) + plane(1) + plane(3)
    for n in range(4):
        arrived(FP + n, block(2, PASS_P[n]))
        arrived(FM + n, block(2, PASS_M[n]))
    found += plane(2)
    product = dot_nt(left[:, 0:R], sbuf[0])
    for d in range(1, X):
        arrived(GX + d - 1, sbuf.at[X - d])
        product += dot_nt(left[:, (X - d) * R:(X - d + 1) * R], sbuf[X - d])
    newm[...] = mbuf[...] - product[:R]
    keys[...] = ((found - product[R:]) * D ** -0.5).astype(BF)

    for copy in sent:
        copy.wait_send()


def store(res, newm, keys, res_out, newm_out, keys_out, sem):
    copies = [
        pltpu.make_async_copy(res, res_out, sem.at[0]),
        pltpu.make_async_copy(newm, newm_out, sem.at[1]),
        pltpu.make_async_copy(keys, keys_out, sem.at[2]),
    ]
    for copy in copies:
        copy.start()
    for copy in copies:
        copy.wait()


def body(momentum, gradient, masters, tokens, freq_index):
    hbm = pl.BlockSpec(memory_space=pl.ANY)
    vmem = pl.BlockSpec(memory_space=pltpu.VMEM)
    held = pl.pallas_call(
        kernel,
        out_shape=(
            pltpu.VMEM((1, D, CB), F32),
            pltpu.VMEM((R, CB), F32),
            pltpu.VMEM((T, CB), BF),
        ),
        in_specs=[hbm] * 5,
        out_specs=(vmem, vmem, vmem),
        scratch_shapes=[
            pltpu.VMEM((D, CB), BF),
            pltpu.VMEM((H, K), BF),
            pltpu.VMEM((2 * CB, H), BF),
            pltpu.VMEM((2 * CB, K), BF),
            pltpu.VMEM((X, CB, R), BF),
            pltpu.VMEM((X - 1, CB, R), BF),
            pltpu.VMEM((Z, 16, R), BF),
            pltpu.VMEM((Z - 1, 16, R), BF),
            pltpu.VMEM((X, CB, R), BF),
            pltpu.VMEM((8, T, 1024), BF),
            pltpu.VMEM((2 * T, H), BF),
            pltpu.VMEM((R + T, K), BF),
            pltpu.VMEM((X, Z, R, CB), BF),
            pltpu.VMEM((R, CB), F32),
            pltpu.VMEM((1, K), jnp.int32),
            pltpu.VMEM((1, K), jnp.int32),
            pltpu.VMEM((R, R), F32),
            pltpu.VMEM((2, 64, 128), F32),
            pltpu.VMEM((2, 64, 128), F32),
            pltpu.SemaphoreType.DMA((19,)),
            pltpu.SemaphoreType.DMA((MSGS,)),
            pltpu.SemaphoreType.DMA((MSGS,)),
        ],
        compiler_params=pltpu.CompilerParams(
            collective_id=0, has_side_effects=True, vmem_limit_bytes=56 * 1024 * 1024),
    )(momentum, gradient, masters, tokens, freq_index)
    return pl.pallas_call(
        store,
        out_shape=(
            jax.ShapeDtypeStruct((1, D, CB), F32),
            jax.ShapeDtypeStruct((R, CB), F32),
            jax.ShapeDtypeStruct((T, CB), BF),
        ),
        in_specs=[vmem] * 3,
        out_specs=(hbm, hbm, hbm),
        scratch_shapes=[pltpu.SemaphoreType.DMA((3,))],
        compiler_params=pltpu.CompilerParams(vmem_limit_bytes=4 * 1024 * 1024),
    )(*[pltpu.with_memory_space_constraint(a, pltpu.VMEM) for a in held])


def solution(mesh):
    return jax.shard_map(
        body,
        mesh=mesh,
        in_specs=(
            P("dp", None, "tensor"),
            P("dp", None, "tensor"),
            P("dp", "tensor"),
            P("dp", "tensor"),
            P("tensor", None),
        ),
        out_specs=(P("dp", None, "tensor"), P("dp", "tensor"), P("dp", "tensor")),
        check_vma=False,
    )
```
